256 devices in a mesh: seq: 32 (over z, x), head: 8 (over y, core).
Axes of the slice: x: 4, y: 4, z: 8, core: 2. Of those that a mesh axis runs over, the one named last changes fastest.
Arguments:
- queries: bfloat16 [32768, 2048], P('seq', 'head'), may hold values from -6 to 6
- keys: bfloat16 [32768, 2048], P('seq', 'head'), may hold values from -6 to 6
- values: bfloat16 [32768, 2048], P('seq', 'head'), may hold values from -6 to 6
- router_weight: bfloat16 [2048, 32], replicated, may hold values from -0.078125 to 0.078125
- gate_weight: bfloat16 [32, 2048, 512], P('seq'), may hold values from -0.125 to 0.125
- up_weight: bfloat16 [32, 2048, 512], P('seq'), may hold values from -0.125 to 0.125
- down_weight: bfloat16 [32, 2048, 512], P('seq'), may hold values from -0.5 to 0.5
- route_ids: int32 [32768, 8], P(('seq', 'head')), may hold values from 0 to 31, all different within a row; in each aligned block of 128 rows (0 to 127, 128 to 255, ...) at most 40 rows name the same one
Outputs:
- scored: bfloat16 [32768, 2048], P(('seq', 'head'))
The draws below stay inside these ranges and needn't reach their ends.
Inputs may be any that keep to these rules, and one draw needn't show every extreme that they name: `route_ids`: in every aligned block of 128 rows (the rows of one device) each row names 8 different experts and no expert is named by more than 40 rows; some expert is named by exactly 40 rows of some block in every draw.
All inputs are finite; a program needn't handle non-finite values.
Results may differ from the reference program's by a relative error of at most 0.011.
Values may be sent and summed in bfloat16 or wider, within the bound.
A program may use at most 128 MiB of HBM per device.

```python
import math
import jax
import jax.numpy as jnp
import numpy as np
from jax import lax

H = 16
HD = 128
D = 2048
FF = 512
EXPERTS = 32
TOPK = 8
TOK_DEV = 1024
TOKENS = 32768
ROWS = 128
CAP = 40
N_SEQ = 32


def steps_of(own_key, shape, split, smallest, largest):
    loudness = 1.0
    for axis_at, parts in split:
        draws = jax.random.uniform(jax.random.fold_in(jax.random.fold_in(own_key, 6), axis_at), (parts,), jnp.float32, smallest / len(split), largest / len(split))
        loudness = loudness * jnp.repeat(jnp.exp(draws), shape[axis_at] // parts).reshape((-1,) + (1,) * (len(shape) - 1 - axis_at))
    return loudness


def routed_block(own_key, own, number, rows, count, top, most, lean):
    sequence = jax.random.permutation(own_key, count)
    heavy_load, ordinary = load_shares(count, rows * top, most, lean, True), load_shares(count, rows * top, most, lean, False)
    places = jnp.arange(count)

    def named(lengths, rotation):
        used = int((lengths > 0).sum())
        fixed = max(1, used // 4)
        shifted = fixed + (places - fixed + rotation * (used - fixed)) % max(1, count - fixed)
        return jnp.zeros((count,), jnp.int32).at[sequence[jnp.where(places < fixed, places, shifted)]].set(jnp.asarray(lengths, jnp.int32))

    lengths = jnp.where(number % 4 == 0, named(heavy_load, number // 4), named(ordinary, number - number // 4 - 1))
    mixed = jax.random.permutation(jax.random.fold_in(own, 3), count)
    source_of, sink = mixed[0:count // 2 * 2:2], mixed[1:count // 2 * 2:2]
    slack = jnp.minimum(lengths[source_of] - 1, most - lengths[sink]) // 2
    slack = jnp.where((source_of == sequence[0]) | (sink == sequence[0]) | (lengths[sink] == 0), 0, jnp.maximum(slack, 0))
    shifted = jax.random.randint(jax.random.fold_in(own, 4), (count // 2,), 0, 1 << 20) % (slack + 1)
    lengths = lengths.at[source_of].add(-shifted).at[sink].add(shifted)
    labels = jnp.searchsorted(jnp.cumsum(lengths), jnp.arange(rows * top), side="right").astype(jnp.int32)
    listing = labels.reshape(top, rows).T
    listing = listing[jax.random.permutation(jax.random.fold_in(own, 1), rows)]
    rotation = jax.random.randint(jax.random.fold_in(own, 2), (rows, 1), 0, top)
    return jnp.take_along_axis(listing, (jnp.arange(top)[None, :] + rotation) % top, axis=1)


def load_shares(count, total, bound, skew, full):
    weights = [(1 << 20) // math.isqrt(grade ** skew) + 1 for grade in range(1, count + 1)]
    largest = bound if full else min(bound, max(-(-total // count), total * weights[0] // sum(weights)))
    least = 1 if total - largest >= count - 1 else 0
    counts, rest = [largest] + [least] * (count - 1), total - largest - least * (count - 1)
    while rest > 0:
        movable = [i for i in range(1, count) if counts[i] < largest] or [i for i in range(1, count) if counts[i] < bound]
        whole, remaining = sum([weights[i] for i in movable]), rest
        for i in movable:
            addition = min(bound - counts[i], max(1, remaining * weights[i] // whole), rest)
            counts[i] = counts[i] + addition
            rest = rest - addition
    return np.array(counts)


def bell_draw(rng, dims, width, reach, cuts=(), kind=jnp.bfloat16):
    array = width * jax.random.normal(rng, dims, jnp.float32)
    if cuts:
        array = array * steps_of(rng, dims, cuts, -0.22, 0.18)
    return jnp.clip(array, -reach, reach).astype(kind)


def setup_inputs(seed: int = 0) -> dict:
    key_of = jax.random.split(jax.random.key(seed), 9)
    queries = bell_draw(key_of[0], (TOKENS, D), 1.0, 6.0, ((0, 32), (1, 8)))
    keys = bell_draw(key_of[1], (TOKENS, D), 1.0, 6.0, ((0, 32), (1, 8)))
    values = bell_draw(key_of[2], (TOKENS, D), 1.0, 6.0, ((0, 32), (1, 8)))
    router_weight = bell_draw(key_of[3], (D, EXPERTS), (3 * D) ** -0.5, 0.078125)
    gate_weight = bell_draw(key_of[4], (EXPERTS, D, FF), D ** -0.5, 0.125, ((0, 32),))
    up_weight = bell_draw(key_of[5], (EXPERTS, D, FF), D ** -0.5, 0.125, ((0, 32),))
    down_weight = bell_draw(key_of[6], (EXPERTS, D, FF), (FF // 4) ** -0.5, 0.5, ((0, 32),))
    route_ids_keys = jax.random.split(jax.random.fold_in(key_of[7], 1), TOKENS // ROWS)
    route_ids_turns = jax.random.permutation(jax.random.fold_in(key_of[7], 3), TOKENS // ROWS)
    route_ids = jax.vmap(lambda own, number: routed_block(jax.random.fold_in(key_of[7], 2), own, number, ROWS, EXPERTS, TOPK, CAP, 1))(route_ids_keys, route_ids_turns).reshape((TOKENS, TOPK))
    return dict(queries=queries, keys=keys, values=values, router_weight=router_weight, gate_weight=gate_weight, up_weight=up_weight, down_weight=down_weight, route_ids=route_ids)


epsilon = 1e-06

def slot_numbers(expert_ids, experts):
    blocks, block_rows, top_count = expert_ids.shape
    flat_ids = expert_ids.reshape(blocks, block_rows * top_count)
    onehot = (flat_ids[:, :, None] == jnp.arange(experts, dtype=jnp.int32)[None, None, :]).astype(jnp.int32)
    before = jnp.cumsum(onehot, axis=1) - onehot
    return lax.optimization_barrier(jnp.sum(before * onehot, axis=2)).reshape(blocks * block_rows, top_count).astype(jnp.int32)

def route_weights(logits, expert_ids):
    experts = logits.shape[-1]
    chosen = expert_ids[..., None] == jnp.arange(experts, dtype=jnp.int32)
    gate_score = lax.optimization_barrier(jnp.sum(jnp.where(chosen, jax.nn.sigmoid(logits)[..., None, :], 0.0), axis=-1))
    return gate_score / lax.optimization_barrier(jnp.sum(gate_score, axis=-1, keepdims=True))

def reference(queries, keys, values, router_weight, gate_weight, up_weight, down_weight, route_ids):
    high = lax.Precision.HIGHEST
    query_blocks = queries.reshape(N_SEQ, TOK_DEV, H, HD)
    key_blocks = keys.reshape(N_SEQ, TOK_DEV, H, HD)
    value_blocks = values.reshape(N_SEQ, TOK_DEV, H, HD)
    causal = jnp.arange(TOK_DEV)[:, None] >= jnp.arange(TOK_DEV)[None, :]

    def block_step(running_state, block_data):
        query_b, key_b, value_b = block_data
        query_f = query_b.astype(jnp.float32)
        key_f = key_b.astype(jnp.float32)
        value_f = value_b.astype(jnp.float32)
        scores = jnp.einsum('thd,shd->hts', query_f, key_f, precision=high)
        scores = jnp.where(causal[None], scores, 0.0).astype(jnp.bfloat16)
        within = jnp.einsum('hts,she->the', scores.astype(jnp.float32), value_f, precision=high)
        carried_part = jnp.einsum('thd,hde->the', query_f, running_state, precision=high)
        attention = within + carried_part
        normed = attention * lax.rsqrt(lax.optimization_barrier(jnp.mean(attention * attention, axis=-1, keepdims=True)) + epsilon)
        block_state = jnp.einsum('thd,the->hde', key_f, value_f, precision=high)
        return (running_state + block_state, normed.astype(jnp.bfloat16))
    _, normed = lax.scan(block_step, jnp.zeros((H, HD, HD), jnp.float32), (query_blocks, key_blocks, value_blocks))
    normed = normed.reshape(TOKENS, D)
    logits = jnp.dot(normed, router_weight, preferred_element_type=jnp.float32)
    weights = route_weights(logits, route_ids)
    blocks = TOKENS // ROWS
    slot_rank = slot_numbers(route_ids.reshape(blocks, ROWS, TOPK), EXPERTS)
    token_ids = jnp.broadcast_to(jnp.arange(TOKENS, dtype=jnp.int32)[:, None], (TOKENS, TOPK))
    column = (token_ids // ROWS * CAP + slot_rank).astype(jnp.int32)
    expert_table = jnp.full((EXPERTS, blocks * CAP), -1, jnp.int32).at[route_ids, column].set(token_ids)

    def run_expert(expert_item):
        gate_e, up_e, down_e, chosen = expert_item
        present = chosen >= 0
        picked_rows = normed[jnp.maximum(chosen, 0)]
        expert_rows = jnp.where(present[:, None], picked_rows, jnp.zeros_like(picked_rows))
        gate_part = jnp.dot(expert_rows, gate_e, preferred_element_type=jnp.float32)
        up_part = jnp.dot(expert_rows, up_e, preferred_element_type=jnp.float32)
        hidden = (jax.nn.silu(gate_part) * up_part).astype(jnp.bfloat16)
        return jnp.dot(hidden, down_e.T, preferred_element_type=jnp.float32).astype(jnp.bfloat16)
    produced = lax.map(run_expert, (gate_weight, up_weight, down_weight, expert_table))
    picked = produced[route_ids, column].astype(jnp.float32)
    return lax.optimization_barrier(jnp.sum(weights[..., None] * picked, axis=1)).astype(jnp.bfloat16)
```

```python
import jax
import jax.numpy as jnp
from jax import lax
from jax.sharding import PartitionSpec as P

HD = 128


epsilon = 1e-06


def entering(value, axis, combine, identity):
    devices, mine = (lax.axis_size(axis), lax.axis_index(axis))
    everything = lax.all_gather(value, axis)
    start = jnp.broadcast_to(jnp.asarray(identity, value.dtype), value.shape)

    def hop(k, before):
        reached = k < mine
        new = combine(before, everything[k])
        return jnp.where(reached, new, before)

    return lax.fori_loop(0, devices, hop, start)


def add_states(earlier, later):
    return earlier + later


def route_places(expert_ids, experts):
    blocks, block_rows, top_count = expert_ids.shape
    flat_ids = expert_ids.reshape(blocks, block_rows * top_count)
    pairs = block_rows * top_count
    place = jnp.arange(pairs, dtype=jnp.int32)
    same = (flat_ids[:, :, None] == flat_ids[:, None, :]) & (place[None, :, None] > place[None, None, :])
    slot_rank = jnp.sum(same.astype(jnp.int32), axis=2)
    return (slot_rank * experts + flat_ids).reshape(blocks, block_rows, top_count)


def route_weights(logits, expert_ids):
    experts = logits.shape[-1]
    chosen = expert_ids[..., None] == jnp.arange(experts, dtype=jnp.int32)
    gate_score = jnp.sum(jnp.where(chosen, jax.nn.sigmoid(logits)[..., None, :], 0.0), axis=-1)
    return gate_score / jnp.sum(gate_score, axis=-1, keepdims=True)


def dispatch_matrix(places, slots_total):
    targets = jnp.arange(slots_total, dtype=jnp.int32)
    matches = jnp.any(places[:, None, :, :] == targets[None, :, None, None], axis=-1)
    return matches.astype(jnp.bfloat16)


def body(queries, keys, values, router_weight, gate_weight, up_weight, down_weight, route_ids):
    tok_dev, local_width = queries.shape
    heads_here = local_width // HD
    block_rows, top_count = route_ids.shape
    experts = router_weight.shape[1]
    capacity = min(block_rows, (block_rows * top_count * 5 + 4 * experts - 1) // (4 * experts))
    query_heads = queries.reshape(tok_dev, heads_here, HD)
    key_heads = keys.reshape(tok_dev, heads_here, HD)
    value_heads = values.reshape(tok_dev, heads_here, HD)
    local_state = jnp.einsum(
        "thd,the->hde", key_heads, value_heads, preferred_element_type=jnp.float32
    )
    carried = entering(local_state, "seq", add_states, jnp.zeros_like(local_state))
    scores = jnp.einsum("thd,shd->hts", query_heads, key_heads, preferred_element_type=jnp.float32)
    causal = jnp.arange(tok_dev)[:, None] >= jnp.arange(tok_dev)[None, :]
    scores = jnp.where(causal[None], scores, 0.0).astype(jnp.bfloat16)
    within = jnp.einsum("hts,she->the", scores, value_heads, preferred_element_type=jnp.float32)
    carried_part = jnp.einsum(
        "thd,hde->the", query_heads.astype(jnp.float32), carried, precision=lax.Precision.HIGHEST
    )
    attention = within + carried_part
    normed = attention * lax.rsqrt(
        jnp.mean(attention * attention, axis=-1, keepdims=True) + epsilon
    )
    normed = normed.astype(jnp.bfloat16).reshape(tok_dev, local_width)
    slots_total = capacity * experts
    token_rows = lax.all_to_all(normed, "head", split_axis=0, concat_axis=1, tiled=True)
    logits = jnp.dot(token_rows, router_weight, preferred_element_type=jnp.float32)
    weights = route_weights(logits, route_ids)
    block_places = route_places(route_ids[None], experts)
    selector = dispatch_matrix(block_places, slots_total)
    packed = jnp.einsum(
        "jcr,jrf->jcf", selector, token_rows[None], preferred_element_type=jnp.float32
    )
    packed = packed.astype(jnp.bfloat16).reshape(capacity, experts, token_rows.shape[1])
    arrived = lax.all_to_all(packed, "seq", split_axis=1, concat_axis=0, tiled=True)
    places = block_places[0]
    gate_part = jnp.einsum("med,edf->mef", arrived, gate_weight, preferred_element_type=jnp.float32)
    up_part = jnp.einsum("med,edf->mef", arrived, up_weight, preferred_element_type=jnp.float32)
    hidden = (jax.nn.silu(gate_part) * up_part).astype(jnp.bfloat16)
    produced = jnp.einsum(
        "mef,edf->med", hidden, down_weight, preferred_element_type=jnp.float32
    ).astype(jnp.bfloat16)
    returned = lax.all_to_all(produced, "seq", split_axis=0, concat_axis=1, tiled=True)
    model_width = returned.shape[2]
    flat_places = places.reshape(block_rows * top_count)
    picked = jnp.take(returned.reshape(slots_total, model_width), flat_places, axis=0).astype(
        jnp.float32
    )
    picked = picked.reshape(block_rows, top_count, model_width)
    return jnp.sum(weights[..., None] * picked, axis=1).astype(jnp.bfloat16)


def solution(mesh):
    in_specs = (
        P("seq", "head"),
        P("seq", "head"),
        P("seq", "head"),
        P(),
        P("seq", None, None),
        P("seq", None, None),
        P("seq", None, None),
        P(("seq", "head"), None),
    )
    out_specs = P(("seq", "head"), None)
    return jax.shard_map(body, mesh=mesh, in_specs=in_specs, out_specs=out_specs, check_vma=False)
```

```python
import itertools

import jax
import jax.numpy as jnp
from jax import lax
from jax.experimental import pallas as pl
from jax.experimental.pallas import tpu as pltpu
from jax.sharding import PartitionSpec as P

HD = 128
NX, NZ, NY, NC = 4, 8, 4, 2
CAP = 40
epsilon = 1e-06
BF, F32 = jnp.bfloat16, jnp.float32
MESH = pl.DeviceIdType.MESH
NN, NT, TN = (((1,), (0,)), ((), ())), (((1,), (1,)), ((), ())), (((0,), (0,)), ((), ()))
FLOWS = 128


def dot(a, b, dims=NN):
    return lax.dot_general(a, b, dims, preferred_element_type=F32)


def kernel(q_hbm, k_hbm, v_hbm, rwt, g_hbm, u_hbm, d_hbm, idst, out_ref,
           qv, kv, vv, att, nrm, landed, tok, wv, xs, ys, part, rr, ll,
           st_out, st_in, tot, zs_out, zs_in, cz, car, meta_out, meta_in,
           ssem, rsem, lsem):
    seq, head = lax.axis_index("seq"), lax.axis_index("head")
    z, x = seq // NX, seq % NX
    y, c = head // NC, head % NC
    ids = itertools.count()
    sends = []

    def at_z(k):
        return lax.rem(z + k, NZ) * NX + x

    def at_x(k):
        return z * NX + lax.rem(x + k, NX)

    def at_h(k):
        return lax.rem(head + k, NY * NC)

    def at_y(k):
        return lax.rem(y + k, NY) * NC + c

    other_core = y * NC + (1 - c)

    def push(src, dst, to_seq, to_head):
        i = next(ids)
        cp = pltpu.make_async_remote_copy(
            src_ref=src, dst_ref=dst, send_sem=ssem.at[i], recv_sem=rsem.at[i],
            device_id=(to_seq, to_head), device_id_type=MESH)
        cp.start()
        sends.append(cp)
        return cp

    loads = [pltpu.make_async_copy(src, dst, lsem.at[i])
             for i, (src, dst) in enumerate(((k_hbm, kv), (v_hbm, vv), (q_hbm, qv)))]
    for cp in loads:
        cp.start()
    own = [pltpu.make_async_copy(src, wv.at[0, m], lsem.at[3 + m])
           for m, src in enumerate((g_hbm, u_hbm, d_hbm))]
    for cp in own:
        cp.start()

    barrier = pltpu.get_barrier_semaphore()
    partners = ([(at_x(k), head) for k in range(1, NX)] + [(at_z(k), head) for k in range(1, NZ)]
                + [(seq, at_h(k)) for k in range(1, NY * NC)])
    for to in partners:
        pl.semaphore_signal(barrier, inc=1, device_id=to, device_id_type=MESH)
    pl.semaphore_wait(barrier, len(partners))

    quarter = 2 * lax.rem(y, 2) + c
    across = 2 * (1 - lax.rem(y, 2)) + c
    hbm = (g_hbm, u_hbm, d_hbm)

    def x_send(m):
        src = hbm[m].at[quarter]
        return (push(src, wv.at[3, m, quarter], at_x(1), head), push(src, wv.at[1, m, quarter], at_x(3), head))

    def lo_hi(j, m, base):
        return wv.at[j, m, base, 0], wv.at[j, m, base, 1]

    def spread(j, m):
        lo, hi = lo_hi(j, m, quarter)
        full = wv.at[j, m, quarter]
        return (push(lo, lo, seq, at_y(1)), push(hi, hi, seq, at_y(3)), push(full, full, seq, other_core))

    def x_event(m, flows):
        right, left = flows
        right.wait_recv()
        lo, _ = lo_hi(3, m, quarter)
        f_right = push(lo, wv.at[2, m, quarter, 0], at_x(1), head)
        s3 = spread(3, m)
        left.wait_recv()
        _, hi = lo_hi(1, m, quarter)
        f_left = push(hi, wv.at[2, m, quarter, 1], at_x(3), head)
        s1 = spread(1, m)
        return (f_right, f_left), {3: s3, 1: s1}

    def f_event(m, flows):
        for cp in flows:
            cp.wait_recv()
        return spread(2, m)

    def y_event(j, m, flows):
        flows[0].wait_recv()
        flows[1].wait_recv()
        full = wv.at[j, m, across]
        return push(full, full, seq, other_core)

    xf = {0: x_send(0), 1: x_send(1)}
    fwd, spr, cor = {}, {}, {}

    def do_x(m):
        fwd[m], s = x_event(m, xf[m])
        spr[(3, m)], spr[(1, m)] = s[3], s[1]

    def do_y(j, m):
        cor[(j, m)] = y_event(j, m, spr[(j, m)])

    def do_f(m):
        spr[(2, m)] = f_event(m, fwd[m])

    def ready(j, m):
        if j == 0:
            own[m].wait()
        else:
            spr[(j, m)][2].wait_recv()
            cor[(j, m)].wait_recv()

    for cp in loads:
        cp.wait()
    for h in range(2):
        cols = slice(h * HD, (h + 1) * HD)
        s = dot(kv[:, cols], vv[:, cols], TN)
        tot[cols, :] = s
        st_out[cols, :] = s.astype(BF)
    st = [push(st_out, st_in.at[k - 1], at_x(k), head) for k in range(1, NX)]

    for h in range(2):
        cols = slice(h * HD, (h + 1) * HD)
        for i in range(4):
            qi = qv[i * 256:(i + 1) * 256, cols]
            acc = jnp.zeros((256, HD), F32)
            for j in range(i + 1):
                s = dot(qi, kv[j * 256:(j + 1) * 256, cols], NT)
                if i == j:
                    keep = (lax.broadcasted_iota(jnp.int32, (256, 256), 0)
                            >= lax.broadcasted_iota(jnp.int32, (256, 256), 1))
                    s = jnp.where(keep, s, 0.0)
                acc = acc + dot(s.astype(BF), vv[j * 256:(j + 1) * 256, cols])
            att[i * 256:(i + 1) * 256, cols] = acc

    before = jnp.zeros((2 * HD, HD), F32)
    total = tot[...]
    for k in range(1, NX):
        st[k - 1].wait_recv()
        came = st_in[k - 1].astype(F32)
        total = total + came
        before = before + came * (x >= k).astype(F32)
    tot[...] = total
    mine = pl.ds(pl.multiple_of(x * 64, 64), 64)
    zs_out[...] = tot[mine, :].astype(BF)
    zs = [push(zs_out, zs_in.at[k - 1], at_z(k), head) for k in range(1, NZ)]
    zq = jnp.zeros((64, HD), F32)
    for k in range(1, NZ):
        zs[k - 1].wait_recv()
        zq = zq + zs_in[k - 1].astype(F32) * (z >= k).astype(F32)
    cz[x] = zq.astype(BF)
    cs = [push(cz.at[x], cz.at[x], at_x(k), head) for k in range(1, NX)]
    do_x(0)
    xf[2] = x_send(2)
    for cp in cs:
        cp.wait_recv()
    carried = before + cz[...].astype(F32).reshape(2 * HD, HD)
    high = carried.astype(BF)
    car[0] = high
    car[1] = (carried - high.astype(F32)).astype(BF)

    a2a = []
    for k in range(NY * NC):
        owner = pl.ds(pl.multiple_of(at_h(k) * 128, 128), 128)
        for h in range(2):
            cols = slice(h * HD, (h + 1) * HD)
            qi = qv[owner, cols]
            a = att[owner, cols] + dot(qi, car[0, cols, :]) + dot(qi, car[1, cols, :])
            scale = lax.rsqrt(jnp.mean(a * a, axis=1, keepdims=True) + epsilon)
            nrm[k, :, cols] = (a * scale).astype(BF)
        if k > 0:
            a2a.append(push(nrm.at[k], landed.at[k - 1], seq, at_h(k)))
    do_x(1)
    for k in range(NY * NC):
        if k > 0:
            a2a[k - 1].wait_recv()
        hcols = pl.ds(pl.multiple_of(lax.rem(head + NY * NC - k, NY * NC) * 2 * HD, 2 * HD), 2 * HD)
        tok[0, 0, :, :, hcols] = (nrm[0] if k == 0 else landed[k - 1]).reshape(2, 64, 2 * HD)

    def half(ref, o, b):
        return ref.at[o // 2, o % 2, b]

    def ag(src, b, right):
        dst = (src + 7) % 8 if right else (src + 1) % 8
        return push(half(tok, src, b), half(tok, dst, b), at_z(1 if right else 7), head)

    ag_r, ag_l = {}, {}
    for b in range(2):
        ag_r[(7, b)] = ag(0, b, True)
        ag_l[(1, 1 - b)] = ag(0, 1 - b, False)

    lt = dot(rwt[...], tok[0, 0].reshape(128, rwt.shape[1]), NT)
    experts = lt.shape[0]
    number = lax.broadcasted_iota(jnp.int32, (experts, 128), 0)
    chosen = jnp.zeros((experts, 128), F32)
    for k in range(idst.shape[0]):
        chosen = chosen + jnp.where(number == idst[k:k + 1, :], 1.0, 0.0)
    score = jnp.where(chosen > 0.5, 1.0 / (1.0 + jnp.exp(-lt)), 0.0)
    weight = score / jnp.sum(score, axis=0, keepdims=True)
    earlier = (lax.broadcasted_iota(jnp.int32, (128, 128), 0)
               < lax.broadcasted_iota(jnp.int32, (128, 128), 1))
    rank = dot(chosen.astype(BF), jnp.where(earlier, 1.0, 0.0).astype(BF))
    rank = jnp.where(chosen > 0.5, rank, -1000.0)
    for p in range(NZ):
        meta_out[p, 0:NX, :] = rank[p * NX:(p + 1) * NX, :]
        meta_out[p, NX:2 * NX, :] = weight[p * NX:(p + 1) * NX, :]
    mt = [push(meta_out.at[lax.rem(z + k, NZ)], meta_in.at[8 - k], at_z(k), head) for k in range(1, NZ)]
    meta_in[0] = meta_out[z]

    def forward(o_r, o_l, b):
        ag_r[(o_r, b)].wait_recv()
        if not (o_r == 5 and b == 1):
            ag_r[(o_r - 1, b)] = ag(o_r, b, True)
        ag_l[(o_l, 1 - b)].wait_recv()
        if not (o_l == 3 and 1 - b == 0):
            ag_l[(o_l + 1, 1 - b)] = ag(o_l, 1 - b, False)

    slots = 2 * CAP

    def picks(pair, j):
        xj = lax.rem(x + j, NX)
        r0 = meta_in[2 * pair, pl.ds(xj, 1), :]
        r1 = meta_in[2 * pair + 1, pl.ds(xj, 1), :] + float(CAP)
        r = jnp.concatenate([r0, r1], axis=1)
        return lax.broadcasted_iota(jnp.int32, (slots, 256), 0).astype(F32) == r

    def picked_weight(pair, j):
        xj = lax.rem(x + j, NX)
        w = jnp.concatenate([meta_in[2 * pair, pl.ds(NX + xj, 1), :],
                             meta_in[2 * pair + 1, pl.ds(NX + xj, 1), :]], axis=1)
        return jnp.sum(jnp.where(picks(pair, j), w, 0.0), axis=1, keepdims=True)

    def all_picks(pair):
        return jnp.concatenate([jnp.where(picks(pair, j), 1.0, 0.0) for j in range(NX)], axis=0).astype(BF)

    def gather(lp, pair):
        p = all_picks(pair)
        for n in range(4):
            cols = slice(n * 512, (n + 1) * 512)
            got = dot(p, tok[pair, :, :, :, cols].reshape(256, 512)).astype(BF)
            for j in range(NX):
                xs[j, lp * slots:(lp + 1) * slots, cols] = got[j * slots:(j + 1) * slots, :]

    def whole(j, m):
        return wv[j, m].reshape(2048, 512)

    def expert(j, pairs):
        w = jnp.concatenate([picked_weight(pair, j) for pair in pairs], axis=0)
        rows_in = xs[j]
        gate = dot(rows_in, whole(j, 0))
        up = dot(rows_in, whole(j, 1))
        hidden = (gate / (1.0 + jnp.exp(-gate)) * up * w).astype(BF)
        for n in range(4):
            cols = slice(n * 512, (n + 1) * 512)
            made = dot(hidden, wv[j, 2, n].reshape(512, 512), NT).astype(BF)
            for lp in range(2):
                ys[lp, j * slots:(j + 1) * slots, cols] = made[lp * slots:(lp + 1) * slots, :]

    def combine(lp, pair):
        p = all_picks(pair)
        for n in range(4):
            cols = slice(n * 512, (n + 1) * 512)
            part[pair, :, :, :, cols] = dot(p, ys[lp, :, cols], TN).astype(BF).reshape(2, 2, 64, 512)

    near, far = (0, 3), (1, 2)
    forward(7, 1, 0)
    do_y(3, 0), do_y(1, 0)
    do_f(0)
    forward(7, 1, 1)
    for cp in mt:
        cp.wait_recv()
    gather(0, 0)
    do_x(2)
    do_y(3, 1), do_y(1, 1)
    forward(6, 2, 0)
    do_f(1)
    forward(6, 2, 1)
    gather(1, 3)
    do_y(2, 0)
    do_y(3, 2), do_y(1, 2)
    for m in range(3):
        ready(0, m)
    expert(0, near)
    forward(5, 3, 0)
    do_f(2)
    do_y(2, 1)
    for j in (3, 1):
        for m in range(3):
            ready(j, m)
        expert(j, near)
    forward(5, 3, 1)
    do_y(2, 2)
    for m in range(3):
        ready(2, m)
    expert(2, near)
    combine(0, 0)
    combine(1, 3)
    gather(0, 1)
    ag_r[(4, 0)].wait_recv()
    ag_l[(4, 1)].wait_recv()
    gather(1, 2)
    for j in range(NX):
        expert(j, far)

    def fold(buf, i, o, b):
        def step(r, carry):
            here = pl.ds(pl.multiple_of(r * 16, 16), 16)
            buf[i, here, :] = (buf[i, here, :].astype(F32) + part[o // 2, o % 2, b, here, :].astype(F32)).astype(BF)
            return carry
        lax.fori_loop(0, 4, step, 0)

    combine(1, 2)
    r_in, l_in = {}, {}
    r_in[0] = push(half(part, 4, 0), rr.at[0], at_z(1), head)
    l_in[0] = push(half(part, 4, 1), ll.at[0], at_z(7), head)
    l_in[2] = push(half(part, 5, 0), ll.at[2], at_z(7), head)
    combine(0, 1)
    r_in[2] = push(half(part, 3, 1), rr.at[2], at_z(1), head)
    for i, to, step in ((0, 1, 1), (1, 3, 2), (2, 4, 2), (3, 5, 3), (4, 6, 3)):
        b = {0: 0, 1: 0, 2: 1, 3: 0, 4: 1}[i]
        r_in[i].wait_recv()
        fold(rr, i, 4 - step, b)
        r_in[to] = push(rr.at[i], rr.at[to], at_z(1), head)
        l_in[i].wait_recv()
        fold(ll, i, 4 + step, 1 - b)
        l_in[to] = push(ll.at[i], ll.at[to], at_z(7), head)
    for b, (ri, li) in enumerate(((5, 6), (6, 5))):
        r_in[ri].wait_recv()
        l_in[li].wait_recv()

        def last(r, carry, b=b, ri=ri, li=li):
            here = pl.ds(pl.multiple_of(r * 16, 16), 16)
            there = pl.ds(pl.multiple_of(b * 64 + r * 16, 16), 16)
            out_ref[there, :] = (rr[ri, here, :].astype(F32) + ll[li, here, :].astype(F32)
                                 + part[0, 0, b, here, :].astype(F32)).astype(BF)
            return carry
        lax.fori_loop(0, 4, last, 0)
    for cp in sends:
        cp.wait_send()


def body(queries, keys, values, router_weight, gate_weight, up_weight, down_weight, route_ids):
    tok_dev, width = queries.shape
    block_rows, top_count = route_ids.shape
    dim, hidden = gate_weight.shape[1:]
    anywhere = pl.BlockSpec(memory_space=pl.ANY)
    vmem = pl.BlockSpec(memory_space=pltpu.VMEM)
    V = pltpu.VMEM
    return pl.pallas_call(
        kernel,
        out_shape=jax.ShapeDtypeStruct((block_rows, dim), BF),
        in_specs=[anywhere] * 3 + [vmem] + [anywhere] * 3 + [vmem],
        out_specs=vmem,
        scratch_shapes=[
            V((tok_dev, width), BF), V((tok_dev, width), BF), V((tok_dev, width), BF),
            V((tok_dev, width), F32), V((NY * NC, block_rows, width), BF), V((NY * NC - 1, block_rows, width), BF),
            V((NZ // 2, 2, 2, block_rows // 2, dim), BF),
            V((NX, 3, 4, 2, dim // 8, hidden), BF),
            V((NX, 4 * CAP, dim), BF), V((2, NX * 2 * CAP, dim), BF),
            V((NZ // 2, 2, 2, block_rows // 2, dim), BF),
            V((7, block_rows // 2, dim), BF), V((7, block_rows // 2, dim), BF),
            V((2 * HD, HD), BF), V((NX - 1, 2 * HD, HD), BF), V((2 * HD, HD), F32),
            V((64, HD), BF), V((NZ - 1, 64, HD), BF), V((NX, 64, HD), BF), V((2, 2 * HD, HD), BF),
            V((NZ, 2 * NX, block_rows), F32), V((NZ, 2 * NX, block_rows), F32),
            pltpu.SemaphoreType.DMA((FLOWS,)), pltpu.SemaphoreType.DMA((FLOWS,)),
            pltpu.SemaphoreType.DMA((8,)),
        ],
        compiler_params=pltpu.CompilerParams(
            collective_id=0, has_side_effects=True, vmem_limit_bytes=62 * 1024 * 1024),
        cost_estimate=pl.CostEstimate(flops=10 ** 10, bytes_accessed=10 ** 7, transcendentals=0),
    )(queries, keys, values, router_weight.T, *(w.reshape(4, 2, dim // 8, hidden) for w in (gate_weight, up_weight, down_weight)),
      route_ids.T)


def solution(mesh):
    in_specs = (
        P("seq", "head"),
        P("seq", "head"),
        P("seq", "head"),
        P(),
        P("seq", None, None),
        P("seq", None, None),
        P("seq", None, None),
        P(("seq", "head"), None),
    )
    out_specs = P(("seq", "head"), None)
    return jax.shard_map(body, mesh=mesh, in_specs=in_specs, out_specs=out_specs, check_vma=False)
```

```python
import itertools

import jax
import jax.numpy as jnp
from jax import lax
from jax.experimental import pallas as pl
from jax.experimental.pallas import tpu as pltpu
from jax.sharding import PartitionSpec as P

HD = 128
NX, NZ, NY, NC = 4, 8, 4, 2
CAP = 40
epsilon = 1e-06
BF, F32 = jnp.bfloat16, jnp.float32
MESH = pl.DeviceIdType.MESH
NN, NT, TN = (((1,), (0,)), ((), ())), (((1,), (1,)), ((), ())), (((0,), (0,)), ((), ()))
FLOWS = 160
UNITS, COMMON_U = 32, 2
OWN_U = (UNITS - 2 * COMMON_U) // 4


def dot(a, b, dims=NN):
    return lax.dot_general(a, b, dims, preferred_element_type=F32)


def kernel(q_hbm, k_hbm, v_hbm, rwt, g_hbm, u_hbm, d_hbm, idst, out_ref,
           qv, kv, vv, att, nrm, landed, tok, wv, xs, ys, part, rr, ll,
           st_out, st_in, tot, zs_out, zs_in, cz_out, cz, car, meta_out, meta_in,
           ssem, rsem, lsem):
    seq, head = lax.axis_index("seq"), lax.axis_index("head")
    z, x = seq // NX, seq % NX
    y, c = head // NC, head % NC
    ids = itertools.count()
    sends = []

    def at_z(k):
        return lax.rem(z + k, NZ) * NX + x

    def at_x(k):
        return z * NX + lax.rem(x + k, NX)

    def at_h(k):
        return lax.rem(head + k, NY * NC)

    def at_y(k):
        return lax.rem(y + k, NY) * NC + c

    other_core = y * NC + (1 - c)

    def push(src, dst, to_seq, to_head):
        i = next(ids)
        cp = pltpu.make_async_remote_copy(
            src_ref=src, dst_ref=dst, send_sem=ssem.at[i], recv_sem=rsem.at[i],
            device_id=(to_seq, to_head), device_id_type=MESH)
        cp.start()
        sends.append(cp)
        return cp

    loads = [pltpu.make_async_copy(src, dst, lsem.at[i])
             for i, (src, dst) in enumerate(((k_hbm, kv), (v_hbm, vv), (q_hbm, qv)))]
    for cp in loads:
        cp.start()
    own = [pltpu.make_async_copy(src, wv.at[0, m], lsem.at[3 + m])
           for m, src in enumerate((g_hbm, u_hbm, d_hbm))]
    for cp in own:
        cp.start()

    barrier = pltpu.get_barrier_semaphore()
    partners = ([(at_x(k), head) for k in range(1, NX)] + [(at_z(k), head) for k in range(1, NZ)]
                + [(seq, at_h(k)) for k in range(1, NY * NC)])
    for to in partners:
        pl.semaphore_signal(barrier, inc=1, device_id=to, device_id_type=MESH)
    pl.semaphore_wait(barrier, len(partners))

    quarter = (2 * lax.rem(y, 2) + c) * OWN_U
    across = (2 * (1 - lax.rem(y, 2)) + c) * OWN_U
    common = 4 * OWN_U + c * COMMON_U
    hbm = (g_hbm, u_hbm, d_hbm)

    def part_of(j, m, start, count):
        return wv.at[j, m, pl.ds(start, count)]

    def same(j, m, start, count, to_seq, to_head):
        piece = part_of(j, m, start, count)
        return push(piece, piece, to_seq, to_head)

    def x_send(m, start, count):
        src = hbm[m].at[pl.ds(start, count)]
        return (push(src, part_of(3, m, start, count), at_x(1), head),
                push(src, part_of(1, m, start, count), at_x(3), head))

    def low(j, m):
        return OWN_U // 2 + (j + m) % 2 * (OWN_U % 2)

    def spread(j, m):
        n = low(j, m)
        return (same(j, m, quarter, n, seq, at_y(1)), same(j, m, quarter + n, OWN_U - n, seq, at_y(3)),
                same(j, m, quarter, OWN_U, seq, other_core))

    xf, xc, fwd, fwc, spr, cor, com = {}, {}, {}, {}, {}, {}, {}

    def do_x(m):
        right, left = xf[m]
        n = low(2, m)
        right.wait_recv()
        f_right = push(part_of(3, m, quarter, n), part_of(2, m, quarter, n), at_x(1), head)
        spr[(3, m)] = spread(3, m)
        left.wait_recv()
        f_left = push(part_of(1, m, quarter + n, OWN_U - n), part_of(2, m, quarter + n, OWN_U - n), at_x(3), head)
        spr[(1, m)] = spread(1, m)
        fwd[m] = (f_right, f_left)

    def do_f(m):
        for cp in fwd[m]:
            cp.wait_recv()
        spr[(2, m)] = spread(2, m)

    def do_y(j, m):
        flows = spr[(j, m)]
        flows[0].wait_recv()
        flows[1].wait_recv()
        cor[(j, m)] = same(j, m, across, OWN_U, seq, other_core)

    def do_c(m):
        n = COMMON_U // 2
        right, left = xc[m]
        right.wait_recv()
        f_right = push(part_of(3, m, common, n), part_of(2, m, common, n), at_x(1), head)
        left.wait_recv()
        f_left = push(part_of(1, m, common + n, COMMON_U - n), part_of(2, m, common + n, COMMON_U - n), at_x(3), head)
        for j in (3, 1):
            com[(j, m)] = same(j, m, common, COMMON_U, seq, other_core)
        fwc[m] = (f_right, f_left)

    def do_fc(m):
        for cp in fwc[m]:
            cp.wait_recv()
        com[(2, m)] = same(2, m, common, COMMON_U, seq, other_core)

    def ready(j):
        for m in range(3):
            if j == 0:
                own[m].wait()
            else:
                spr[(j, m)][2].wait_recv()
                cor[(j, m)].wait_recv()
                com[(j, m)].wait_recv()

    for cp in loads:
        cp.wait()
    for h in range(2):
        cols = slice(h * HD, (h + 1) * HD)
        s = dot(kv[:, cols], vv[:, cols], TN)
        for i in range(2):
            tot[2 * h + i] = s[i * 64:(i + 1) * 64, :]
            st_out[2 * h + i] = s[i * 64:(i + 1) * 64, :].astype(BF)
    st = [push(st_out.at[lax.rem(x + k, NX)], st_in.at[k - 1], at_x(k), head) for k in range(1, NX)]

    def intra(h, tiles):
        cols = slice(h * HD, (h + 1) * HD)
        for i in tiles:
            qi = qv[i * 256:(i + 1) * 256, cols]
            acc = jnp.zeros((256, HD), F32)
            for j in range(i + 1):
                s = dot(qi, kv[j * 256:(j + 1) * 256, cols], NT)
                if i == j:
                    keep = (lax.broadcasted_iota(jnp.int32, (256, 256), 0)
                            >= lax.broadcasted_iota(jnp.int32, (256, 256), 1))
                    s = jnp.where(keep, s, 0.0)
                acc = acc + dot(s.astype(BF), vv[j * 256:(j + 1) * 256, cols])
            att[i * 256:(i + 1) * 256, cols] = acc

    intra(0, (0, 1, 2))
    total = tot[x]
    for k in range(1, NX):
        st[k - 1].wait_recv()
        total = total + st_in[k - 1].astype(F32)
    zs_out[...] = total.astype(BF)
    zs = [push(zs_out, zs_in.at[k - 1], at_z(k), head) for k in range(1, NZ)]
    intra(0, (3,))
    intra(1, (0, 1, 2, 3))
    zq = jnp.zeros((64, HD), F32)
    for k in range(1, NZ):
        zs[k - 1].wait_recv()
        zq = zq + zs_in[k - 1].astype(F32) * (z >= k).astype(F32)
    own_state = tot[x]
    for k in range(NX):
        to = lax.rem(x + k, NX)
        entering = zq + own_state * (to > x).astype(F32)
        for i in range(1, NX):
            came_from = lax.rem(x + NX - i, NX)
            entering = entering + st_in[i - 1].astype(F32) * (to > came_from).astype(F32)
        if k == 0:
            cz[x] = entering
        else:
            cz_out[k - 1] = entering
    cs = [push(cz_out.at[k - 1], cz.at[x], at_x(k), head) for k in range(1, NX)]
    for cp in cs:
        cp.wait_recv()
    for m in range(3):
        xf[m] = x_send(m, quarter, OWN_U)
    carried = cz[...].reshape(2 * HD, HD)
    high = carried.astype(BF)
    car[0] = high
    car[1] = (carried - high.astype(F32)).astype(BF)

    a2a = []
    for k in range(NY * NC):
        owner = pl.ds(pl.multiple_of(at_h(k) * 128, 128), 128)
        for h in range(2):
            cols = slice(h * HD, (h + 1) * HD)
            qi = qv[owner, cols]
            a = att[owner, cols] + dot(qi, car[0, cols, :]) + dot(qi, car[1, cols, :])
            scale = lax.rsqrt(jnp.mean(a * a, axis=1, keepdims=True) + epsilon)
            nrm[k, :, cols] = (a * scale).astype(BF)
        if k > 0:
            a2a.append(push(nrm.at[k], landed.at[k - 1], seq, at_h(k)))
    for k in range(NY * NC):
        if k > 0:
            a2a[k - 1].wait_recv()
        hcols = pl.ds(pl.multiple_of(lax.rem(head + NY * NC - k, NY * NC) * 2 * HD, 2 * HD), 2 * HD)
        tok[0, 0, :, :, hcols] = (nrm[0] if k == 0 else landed[k - 1]).reshape(2, 64, 2 * HD)

    def half(ref, o, b):
        return ref.at[o // 2, o % 2, b]

    def ag(src, b, right):
        dst = (src + 7) % 8 if right else (src + 1) % 8
        return push(half(tok, src, b), half(tok, dst, b), at_z(1 if right else 7), head)

    ag_r, ag_l = {}, {}
    for b in range(2):
        ag_r[(7, b)] = ag(0, b, True)
        ag_l[(1, 1 - b)] = ag(0, 1 - b, False)

    lt = dot(rwt[...], tok[0, 0].reshape(128, rwt.shape[1]), NT)
    experts = lt.shape[0]
    number = lax.broadcasted_iota(jnp.int32, (experts, 128), 0)
    chosen = jnp.zeros((experts, 128), F32)
    for k in range(idst.shape[0]):
        chosen = chosen + jnp.where(number == idst[k:k + 1, :], 1.0, 0.0)
    score = jnp.where(chosen > 0.5, 1.0 / (1.0 + jnp.exp(-lt)), 0.0)
    weight = score / jnp.sum(score, axis=0, keepdims=True)
    earlier = (lax.broadcasted_iota(jnp.int32, (128, 128), 0)
               < lax.broadcasted_iota(jnp.int32, (128, 128), 1))
    rank = dot(chosen.astype(BF), jnp.where(earlier, 1.0, 0.0).astype(BF))
    rank = jnp.where(chosen > 0.5, rank, -1000.0)
    for p in range(NZ):
        meta_out[p, 0:NX, :] = rank[p * NX:(p + 1) * NX, :]
        meta_out[p, NX:2 * NX, :] = weight[p * NX:(p + 1) * NX, :]
    mt = [push(meta_out.at[lax.rem(z + k, NZ)], meta_in.at[8 - k], at_z(k), head) for k in range(1, NZ)]
    meta_in[0] = meta_out[z]

    def forward(o_r, o_l, b):
        ag_r[(o_r, b)].wait_recv()
        if not (o_r == 5 and b == 1):
            ag_r[(o_r - 1, b)] = ag(o_r, b, True)
        ag_l[(o_l, 1 - b)].wait_recv()
        if not (o_l == 3 and 1 - b == 0):
            ag_l[(o_l + 1, 1 - b)] = ag(o_l, 1 - b, False)

    slots = 2 * CAP

    def picks(pair, j):
        xj = lax.rem(x + j, NX)
        r0 = meta_in[2 * pair, pl.ds(xj, 1), :]
        r1 = meta_in[2 * pair + 1, pl.ds(xj, 1), :] + float(CAP)
        r = jnp.concatenate([r0, r1], axis=1)
        return lax.broadcasted_iota(jnp.int32, (slots, 256), 0).astype(F32) == r

    def picked_weight(pair, j):
        xj = lax.rem(x + j, NX)
        w = jnp.concatenate([meta_in[2 * pair, pl.ds(NX + xj, 1), :],
                             meta_in[2 * pair + 1, pl.ds(NX + xj, 1), :]], axis=1)
        return jnp.sum(jnp.where(picks(pair, j), w, 0.0), axis=1, keepdims=True)

    def all_picks(pair):
        return jnp.concatenate([jnp.where(picks(pair, j), 1.0, 0.0) for j in range(NX)], axis=0).astype(BF)

    def gather(batch, lp, pair):
        p = all_picks(pair)
        for n in range(4):
            cols = slice(n * 512, (n + 1) * 512)
            got = dot(p, tok[pair, :, :, :, cols].reshape(256, 512)).astype(BF)
            for j in range(NX):
                xs[batch, j, lp * slots:(lp + 1) * slots, cols] = got[j * slots:(j + 1) * slots, :]

    def whole(j, m):
        return wv[j, m].reshape(2048, 512)

    def expert(j, batch, pairs):
        w = jnp.concatenate([picked_weight(pair, j) for pair in pairs], axis=0)
        rows_in = xs[batch, j]
        gate = dot(rows_in, whole(j, 0))
        up = dot(rows_in, whole(j, 1))
        hidden = (gate / (1.0 + jnp.exp(-gate)) * up * w).astype(BF)
        for n in range(4):
            cols = slice(n * 512, (n + 1) * 512)
            made = dot(hidden, wv[j, 2, n * 8:(n + 1) * 8].reshape(512, 512), NT).astype(BF)
            for lp, pair in enumerate(pairs):
                ys[pair, j * slots:(j + 1) * slots, cols] = made[lp * slots:(lp + 1) * slots, :]

    def combine(pair):
        p = all_picks(pair)
        for n in range(4):
            cols = slice(n * 512, (n + 1) * 512)
            part[pair, :, :, :, cols] = dot(p, ys[pair, :, cols], TN).astype(BF).reshape(2, 2, 64, 512)

    near, far = (0, 3), (1, 2)
    do_x(0)
    forward(7, 1, 0)
    forward(7, 1, 1)
    for cp in mt:
        cp.wait_recv()
    gather(0, 0, 0)
    do_x(1)
    do_y(3, 0), do_y(1, 0)
    forward(6, 2, 0)
    forward(6, 2, 1)
    gather(0, 1, 3)
    ready(0)
    do_x(2)
    for m in range(3):
        xc[m] = x_send(m, common, COMMON_U)
    forward(5, 3, 0)
    do_y(3, 1), do_y(1, 1)
    expert(0, 0, near)
    do_f(0)
    forward(5, 3, 1)
    gather(1, 0, 1)
    do_f(1)
    do_y(3, 2), do_y(1, 2)
    do_f(2)
    ag_r[(4, 0)].wait_recv()
    ag_l[(4, 1)].wait_recv()
    gather(1, 1, 2)
    do_c(0), do_c(1), do_c(2)
    do_y(2, 0)
    expert(0, 1, far)
    do_y(2, 1)
    for j in (3, 1):
        ready(j)
        expert(j, 1, far)
        if j == 3:
            do_fc(0), do_fc(1)
    do_y(2, 2)
    do_fc(2)
    expert(3, 0, near)
    ready(2)
    expert(2, 1, far)

    def fold(buf, i, o, b):
        def step(r, carry):
            here = pl.ds(pl.multiple_of(r * 16, 16), 16)
            buf[i, here, :] = (buf[i, here, :].astype(F32) + part[o // 2, o % 2, b, here, :].astype(F32)).astype(BF)
            return carry
        lax.fori_loop(0, 4, step, 0)

    combine(2)
    r_in, l_in = {}, {}
    r_in[0] = push(half(part, 4, 0), rr.at[0], at_z(1), head)
    l_in[0] = push(half(part, 4, 1), ll.at[0], at_z(7), head)
    l_in[2] = push(half(part, 5, 0), ll.at[2], at_z(7), head)
    combine(1)
    r_in[2] = push(half(part, 3, 1), rr.at[2], at_z(1), head)
    for j in (1, 2):
        expert(j, 0, near)
    combine(3)
    combine(0)
    for i, to, step in ((0, 1, 1), (1, 3, 2), (2, 4, 2), (3, 5, 3), (4, 6, 3)):
        b = {0: 0, 1: 0, 2: 1, 3: 0, 4: 1}[i]
        r_in[i].wait_recv()
        fold(rr, i, 4 - step, b)
        r_in[to] = push(rr.at[i], rr.at[to], at_z(1), head)
        l_in[i].wait_recv()
        fold(ll, i, 4 + step, 1 - b)
        l_in[to] = push(ll.at[i], ll.at[to], at_z(7), head)
    for b, (ri, li) in enumerate(((5, 6), (6, 5))):
        r_in[ri].wait_recv()
        l_in[li].wait_recv()

        def last(r, carry, b=b, ri=ri, li=li):
            here = pl.ds(pl.multiple_of(r * 16, 16), 16)
            there = pl.ds(pl.multiple_of(b * 64 + r * 16, 16), 16)
            out_ref[there, :] = (rr[ri, here, :].astype(F32) + ll[li, here, :].astype(F32)
                                 + part[0, 0, b, here, :].astype(F32)).astype(BF)
            return carry
        lax.fori_loop(0, 4, last, 0)
    for cp in sends:
        cp.wait_send()


def body(queries, keys, values, router_weight, gate_weight, up_weight, down_weight, route_ids):
    tok_dev, width = queries.shape
    block_rows, top_count = route_ids.shape
    dim, hidden = gate_weight.shape[1:]
    anywhere = pl.BlockSpec(memory_space=pl.ANY)
    vmem = pl.BlockSpec(memory_space=pltpu.VMEM)
    V = pltpu.VMEM
    return pl.pallas_call(
        kernel,
        out_shape=jax.ShapeDtypeStruct((block_rows, dim), BF),
        in_specs=[anywhere] * 3 + [vmem] + [anywhere] * 3 + [vmem],
        out_specs=vmem,
        scratch_shapes=[
            V((tok_dev, width), BF), V((tok_dev, width), BF), V((tok_dev, width), BF),
            V((tok_dev, width), F32), V((NY * NC, block_rows, width), BF), V((NY * NC - 1, block_rows, width), BF),
            V((NZ // 2, 2, 2, block_rows // 2, dim), BF),
            V((NX, 3, UNITS, dim // UNITS, hidden), BF),
            V((2, NX, 4 * CAP, dim), BF), V((NZ // 2, NX * 2 * CAP, dim), BF),
            V((NZ // 2, 2, 2, block_rows // 2, dim), BF),
            V((7, block_rows // 2, dim), BF), V((7, block_rows // 2, dim), BF),
            V((NX, 64, HD), BF), V((NX - 1, 64, HD), BF), V((NX, 64, HD), F32),
            V((64, HD), BF), V((NZ - 1, 64, HD), BF), V((NX - 1, 64, HD), F32), V((NX, 64, HD), F32), V((2, 2 * HD, HD), BF),
            V((NZ, 2 * NX, block_rows), F32), V((NZ, 2 * NX, block_rows), F32),
            pltpu.SemaphoreType.DMA((FLOWS,)), pltpu.SemaphoreType.DMA((FLOWS,)),
            pltpu.SemaphoreType.DMA((8,)),
        ],
        compiler_params=pltpu.CompilerParams(
            collective_id=0, has_side_effects=True, vmem_limit_bytes=62 * 1024 * 1024),
        cost_estimate=pl.CostEstimate(flops=10 ** 10, bytes_accessed=10 ** 7, transcendentals=0),
    )(queries, keys, values, router_weight.T, *(w.reshape(UNITS, dim // UNITS, hidden) for w in (gate_weight, up_weight, down_weight)),
      route_ids.T)


def solution(mesh):
    in_specs = (
        P("seq", "head"),
        P("seq", "head"),
        P("seq", "head"),
        P(),
        P("seq", None, None),
        P("seq", None, None),
        P("seq", None, None),
        P(("seq", "head"), None),
    )
    out_specs = P(("seq", "head"), None)
    return jax.shard_map(body, mesh=mesh, in_specs=in_specs, out_specs=out_specs, check_vma=False)
```

```python
import itertools

import jax
import jax.numpy as jnp
from jax import lax
from jax.experimental import pallas as pl
from jax.experimental.pallas import tpu as pltpu
from jax.sharding import PartitionSpec as P

HD = 128
NX, NZ, NY, NC = 4, 8, 4, 2
CAP = 40
epsilon = 1e-06
BF, F32 = jnp.bfloat16, jnp.float32
MESH = pl.DeviceIdType.MESH
NN, NT, TN = (((1,), (0,)), ((), ())), (((1,), (1,)), ((), ())), (((0,), (0,)), ((), ()))
FLOWS = 160
UNITS, COMMON_U = 32, 2
OWN_U = (UNITS - 2 * COMMON_U) // 4
ORDER = (0, 4, 1, 7, 2, 6, 3, 5)
PIECES = ((0, 0, 3), (0, 3, OWN_U - 3), (1, 0, OWN_U), (2, 0, OWN_U))


def dot(a, b, dims=NN):
    return lax.dot_general(a, b, dims, preferred_element_type=F32)


def kernel(q_hbm, k_hbm, v_hbm, rwt, g_hbm, u_hbm, d_hbm, idst, out_ref,
           qv, kv, vv, att, nrm, landed, tok, wv, xs, ys, part, rr, ll,
           st_out, st_in, tot, zs_out, zs_in, cz_out, cz, car, meta_out, meta_in,
           ssem, rsem, lsem):
    seq, head = lax.axis_index("seq"), lax.axis_index("head")
    z, x = seq // NX, seq % NX
    y, c = head // NC, head % NC
    ids = itertools.count()
    sends = []

    def at_z(k):
        return lax.rem(z + k, NZ) * NX + x

    def at_x(k):
        return z * NX + lax.rem(x + k, NX)

    def at_h(k):
        return lax.rem(head + k, NY * NC)

    def at_y(k):
        return lax.rem(y + k, NY) * NC + c

    other_core = y * NC + (1 - c)

    def push(src, dst, to_seq, to_head):
        i = next(ids)
        cp = pltpu.make_async_remote_copy(
            src_ref=src, dst_ref=dst, send_sem=ssem.at[i], recv_sem=rsem.at[i],
            device_id=(to_seq, to_head), device_id_type=MESH)
        cp.start()
        sends.append(cp)
        return cp

    loads = [pltpu.make_async_copy(src, dst, lsem.at[i])
             for i, (src, dst) in enumerate(((k_hbm, kv), (v_hbm, vv), (q_hbm, qv)))]
    for cp in loads:
        cp.start()
    own = [pltpu.make_async_copy(src, wv.at[0, m], lsem.at[3 + m])
           for m, src in enumerate((g_hbm, u_hbm, d_hbm))]
    for cp in own:
        cp.start()

    barrier = pltpu.get_barrier_semaphore()
    partners = ([(at_x(k), head) for k in range(1, NX)] + [(at_z(k), head) for k in range(1, NZ)]
                + [(seq, at_h(k)) for k in range(1, NY * NC)])
    for to in partners:
        pl.semaphore_signal(barrier, inc=1, device_id=to, device_id_type=MESH)
    pl.semaphore_wait(barrier, len(partners))

    quarter = (2 * lax.rem(y, 2) + c) * OWN_U
    across = (2 * (1 - lax.rem(y, 2)) + c) * OWN_U
    common = 4 * OWN_U + c * COMMON_U
    hbm = (g_hbm, u_hbm, d_hbm)

    def part_of(j, m, start, count):
        return wv.at[j, m, pl.ds(start, count)]

    def same(j, m, start, count, to_seq, to_head):
        piece = part_of(j, m, start, count)
        return push(piece, piece, to_seq, to_head)

    def x_send(m, start, count):
        src = hbm[m].at[pl.ds(start, count)]
        return (push(src, part_of(3, m, start, count), at_x(1), head),
                push(src, part_of(1, m, start, count), at_x(3), head))

    def low(j, i):
        count = PIECES[i][2]
        return count // 2 + (j + i) % 2 * (count % 2)

    def spread(j, i):
        m, first, count = PIECES[i]
        n, start = low(j, i), quarter + first
        return (same(j, m, start, n, seq, at_y(1)), same(j, m, start + n, count - n, seq, at_y(3)),
                same(j, m, start, count, seq, other_core))

    xf, xc, fwd, fwc, spr, cor, com = {}, {}, {}, {}, {}, {}, {}

    def send(i):
        m, first, count = PIECES[i]
        xf[i] = x_send(m, quarter + first, count)

    def do_x(i):
        m, first, count = PIECES[i]
        right, left = xf[i]
        n, start = low(2, i), quarter + first
        right.wait_recv()
        f_right = push(part_of(3, m, start, n), part_of(2, m, start, n), at_x(1), head)
        spr[(3, i)] = spread(3, i)
        left.wait_recv()
        f_left = push(part_of(1, m, start + n, count - n), part_of(2, m, start + n, count - n), at_x(3), head)
        spr[(1, i)] = spread(1, i)
        fwd[i] = (f_right, f_left)

    def do_f(i):
        for cp in fwd[i]:
            cp.wait_recv()
        spr[(2, i)] = spread(2, i)

    def do_y(j, i):
        m, first, count = PIECES[i]
        flows = spr[(j, i)]
        flows[0].wait_recv()
        flows[1].wait_recv()
        cor[(j, i)] = same(j, m, across + first, count, seq, other_core)

    def do_c(m):
        n = COMMON_U // 2
        right, left = xc[m]
        right.wait_recv()
        f_right = push(part_of(3, m, common, n), part_of(2, m, common, n), at_x(1), head)
        left.wait_recv()
        f_left = push(part_of(1, m, common + n, COMMON_U - n), part_of(2, m, common + n, COMMON_U - n), at_x(3), head)
        for j in (3, 1):
            com[(j, m)] = same(j, m, common, COMMON_U, seq, other_core)
        fwc[m] = (f_right, f_left)

    def do_fc(m):
        for cp in fwc[m]:
            cp.wait_recv()
        com[(2, m)] = same(2, m, common, COMMON_U, seq, other_core)

    def ready(j):
        for m in range(3):
            if j == 0:
                own[m].wait()
            else:
                com[(j, m)].wait_recv()
        if j > 0:
            for i in range(len(PIECES)):
                spr[(j, i)][2].wait_recv()
                cor[(j, i)].wait_recv()

    send(0)
    for cp in loads:
        cp.wait()
    for h in range(2):
        cols = slice(h * HD, (h + 1) * HD)
        s = dot(kv[:, cols], vv[:, cols], TN)
        for i in range(2):
            tot[2 * h + i] = s[i * 64:(i + 1) * 64, :]
            st_out[2 * h + i] = s[i * 64:(i + 1) * 64, :].astype(BF)
    st = [push(st_out.at[lax.rem(x + k, NX)], st_in.at[k - 1], at_x(k), head) for k in range(1, NX)]

    def intra(h, tiles):
        cols = slice(h * HD, (h + 1) * HD)
        for i in tiles:
            qi = qv[i * 256:(i + 1) * 256, cols]
            acc = jnp.zeros((256, HD), F32)
            for j in range(i + 1):
                s = dot(qi, kv[j * 256:(j + 1) * 256, cols], NT)
                if i == j:
                    keep = (lax.broadcasted_iota(jnp.int32, (256, 256), 0)
                            >= lax.broadcasted_iota(jnp.int32, (256, 256), 1))
                    s = jnp.where(keep, s, 0.0)
                acc = acc + dot(s.astype(BF), vv[j * 256:(j + 1) * 256, cols])
            att[i * 256:(i + 1) * 256, cols] = acc

    intra(0, (0, 1, 2))
    total = tot[x]
    for k in range(1, NX):
        st[k - 1].wait_recv()
        total = total + st_in[k - 1].astype(F32)
    zs_out[...] = total.astype(BF)
    zs = [push(zs_out, zs_in.at[k - 1], at_z(k), head) for k in range(1, NZ)]
    send(1)
    intra(0, (3,))
    intra(1, (0, 1, 2, 3))
    do_x(0)
    zq = jnp.zeros((64, HD), F32)
    for k in range(1, NZ):
        zs[k - 1].wait_recv()
        zq = zq + zs_in[k - 1].astype(F32) * (z >= k).astype(F32)
    own_state = tot[x]
    for k in range(NX):
        to = lax.rem(x + k, NX)
        entering = zq + own_state * (to > x).astype(F32)
        for i in range(1, NX):
            came_from = lax.rem(x + NX - i, NX)
            entering = entering + st_in[i - 1].astype(F32) * (to > came_from).astype(F32)
        if k == 0:
            cz[x] = entering
        else:
            cz_out[k - 1] = entering
    cs = [push(cz_out.at[k - 1], cz.at[x], at_x(k), head) for k in range(1, NX)]
    do_x(1)
    for cp in cs:
        cp.wait_recv()
    send(2)
    send(3)
    carried = cz[...].reshape(2 * HD, HD)
    high = carried.astype(BF)
    car[0] = high
    car[1] = (carried - high.astype(F32)).astype(BF)

    a2a = {}
    for b in range(2):
        for k in range(NY * NC):
            owned = pl.ds(pl.multiple_of(at_h(k) * 128 + b * 64, 64), 64)
            for h in range(2):
                cols = slice(h * HD, (h + 1) * HD)
                qi = qv[owned, cols]
                a = att[owned, cols] + dot(qi, car[0, cols, :]) + dot(qi, car[1, cols, :])
                scale = lax.rsqrt(jnp.mean(a * a, axis=1, keepdims=True) + epsilon)
                nrm[b, k, :, cols] = (a * scale).astype(BF)
            if k > 0:
                a2a[(b, k)] = push(nrm.at[b, k], landed.at[b, k - 1], seq, at_h(k))

    def assemble(b):
        for k in range(NY * NC):
            if k > 0:
                a2a[(b, k)].wait_recv()
            hcols = pl.ds(pl.multiple_of(lax.rem(head + NY * NC - k, NY * NC) * 2 * HD, 2 * HD), 2 * HD)
            tok[0, 0, b, :, hcols] = nrm[b, 0] if k == 0 else landed[b, k - 1]

    def half(ref, o, b):
        at = ORDER.index(o)
        return ref.at[at // 2, at % 2, b]

    def ag(src, b, right):
        dst = (src + 7) % 8 if right else (src + 1) % 8
        return push(half(tok, src, b), half(tok, dst, b), at_z(1 if right else 7), head)

    ag_r, ag_l = {}, {}
    for b in range(2):
        assemble(b)
        ag_r[(7, b)] = ag(0, b, True)
        ag_l[(1, b)] = ag(0, b, False)

    do_f(0), do_f(1)
    lt = dot(rwt[...], tok[0, 0].reshape(128, rwt.shape[1]), NT)
    experts = lt.shape[0]
    number = lax.broadcasted_iota(jnp.int32, (experts, 128), 0)
    chosen = jnp.zeros((experts, 128), F32)
    for k in range(idst.shape[0]):
        chosen = chosen + jnp.where(number == idst[k:k + 1, :], 1.0, 0.0)
    score = jnp.where(chosen > 0.5, 1.0 / (1.0 + jnp.exp(-lt)), 0.0)
    weight = score / jnp.sum(score, axis=0, keepdims=True)
    earlier = (lax.broadcasted_iota(jnp.int32, (128, 128), 0)
               < lax.broadcasted_iota(jnp.int32, (128, 128), 1))
    rank = dot(chosen.astype(BF), jnp.where(earlier, 1.0, 0.0).astype(BF))
    rank = jnp.where(chosen > 0.5, rank, -1000.0)
    for p in range(NZ):
        meta_out[p, 0:NX, :] = rank[p * NX:(p + 1) * NX, :]
        meta_out[p, NX:2 * NX, :] = weight[p * NX:(p + 1) * NX, :]
    mt = [push(meta_out.at[lax.rem(z + k, NZ)], meta_in.at[8 - k], at_z(k), head) for k in range(1, NZ)]
    meta_in[0] = meta_out[z]

    def forward(o_r, o_l, b):
        ag_r[(o_r, b)].wait_recv()
        if not (o_r == 5 and b == 1):
            ag_r[(o_r - 1, b)] = ag(o_r, b, True)
        ag_l[(o_l, b)].wait_recv()
        if not (o_l == 3 and b == 0):
            ag_l[(o_l + 1, b)] = ag(o_l, b, False)

    slots = 2 * CAP

    def picks(pair, j):
        xj = lax.rem(x + j, NX)
        r0 = meta_in[ORDER[2 * pair], pl.ds(xj, 1), :]
        r1 = meta_in[ORDER[2 * pair + 1], pl.ds(xj, 1), :] + float(CAP)
        r = jnp.concatenate([r0, r1], axis=1)
        return lax.broadcasted_iota(jnp.int32, (slots, 256), 0).astype(F32) == r

    def picked_weight(pair, j):
        xj = lax.rem(x + j, NX)
        w = jnp.concatenate([meta_in[ORDER[2 * pair], pl.ds(NX + xj, 1), :],
                             meta_in[ORDER[2 * pair + 1], pl.ds(NX + xj, 1), :]], axis=1)
        return jnp.sum(jnp.where(picks(pair, j), w, 0.0), axis=1, keepdims=True)

    def all_picks(pair):
        return jnp.concatenate([jnp.where(picks(pair, j), 1.0, 0.0) for j in range(NX)], axis=0).astype(BF)

    def gather(batch, lp, pair):
        p = all_picks(pair)
        for n in range(4):
            cols = slice(n * 512, (n + 1) * 512)
            got = dot(p, tok[pair, :, :, :, cols].reshape(256, 512)).astype(BF)
            for j in range(NX):
                xs[batch, j, lp * slots:(lp + 1) * slots, cols] = got[j * slots:(j + 1) * slots, :]

    def whole(j, m):
        return wv[j, m].reshape(2048, 512)

    def expert(j, batch, first, pairs):
        w = jnp.concatenate([picked_weight(pair, j) for pair in pairs], axis=0)
        rows_in = xs[batch, j, first * slots:(first + len(pairs)) * slots, :]
        gate = dot(rows_in, whole(j, 0))
        up = dot(rows_in, whole(j, 1))
        hidden = (gate / (1.0 + jnp.exp(-gate)) * up * w).astype(BF)
        for n in range(4):
            cols = slice(n * 512, (n + 1) * 512)
            made = dot(hidden, wv[j, 2, n * 8:(n + 1) * 8].reshape(512, 512), NT).astype(BF)
            for lp, pair in enumerate(pairs):
                ys[pair, j * slots:(j + 1) * slots, cols] = made[lp * slots:(lp + 1) * slots, :]

    def combine(pair):
        p = all_picks(pair)
        for n in range(4):
            cols = slice(n * 512, (n + 1) * 512)
            part[pair, :, :, :, cols] = dot(p, ys[pair, :, cols], TN).astype(BF).reshape(2, 2, 64, 512)

    near, middle, last = (1, 2), (3,), (0,)
    do_x(2)
    forward(7, 1, 0)
    for cp in mt:
        cp.wait_recv()
    forward(7, 1, 1)
    gather(0, 0, 1)
    do_x(3)
    for m in range(3):
        xc[m] = x_send(m, common, COMMON_U)
    forward(6, 2, 0)
    for i in (0, 1):
        do_y(3, i), do_y(1, i), do_y(2, i)
    do_f(2)
    forward(6, 2, 1)
    gather(0, 1, 2)
    ready(0)
    do_f(3)
    expert(0, 0, 0, near)
    forward(5, 3, 0)
    do_y(3, 2), do_y(1, 2)
    do_c(0), do_c(1)
    forward(5, 3, 1)
    do_c(2)
    gather(1, 0, 3)
    do_y(3, 3), do_y(1, 3)
    expert(0, 1, 0, middle)
    ready(3)
    expert(3, 1, 0, middle)
    do_y(2, 2)
    do_fc(0), do_fc(1)
    expert(3, 0, 0, near)
    ready(1)
    expert(1, 1, 0, middle)
    do_fc(2)
    do_y(2, 3)
    expert(1, 0, 0, near)
    ready(2)
    expert(2, 1, 0, middle)
    combine(3)

    def fold(buf, i, o, b):
        def step(r, carry):
            here = pl.ds(pl.multiple_of(r * 16, 16), 16)
            buf[i, here, :] = (buf[i, here, :].astype(F32) + part[ORDER.index(o) // 2, ORDER.index(o) % 2, b, here, :].astype(F32)).astype(BF)
            return carry
        lax.fori_loop(0, 4, step, 0)

    order = ((3, 1), (4, 0), (2, 1), (3, 0), (1, 1), (2, 0), (1, 0))
    r_in, l_in = {}, {}

    def begin(i):
        o, b = order[i]
        r_in[i] = push(half(part, o, b), rr.at[i], at_z(1), head)
        l_in[i] = push(half(part, 8 - o, 1 - b), ll.at[i], at_z(7), head)

    def onward(i):
        o, b = order[i]
        came = order.index((o + 1, b))
        r_in[came].wait_recv()
        fold(rr, came, o, b)
        r_in[i] = push(rr.at[came], rr.at[i], at_z(1), head)
        l_in[came].wait_recv()
        fold(ll, came, 8 - o, 1 - b)
        l_in[i] = push(ll.at[came], ll.at[i], at_z(7), head)

    begin(0)
    ag_r[(4, 0)].wait_recv()
    ag_l[(4, 1)].wait_recv()
    gather(1, 1, 0)
    for j in range(NX):
        expert(j, 1, 1, last)
    combine(0)
    begin(1)
    expert(2, 0, 0, near)
    combine(2)
    onward(2)
    combine(1)
    for i in range(3, 7):
        onward(i)
    for b, (ri, li) in enumerate(((6, 4), (4, 6))):
        r_in[ri].wait_recv()
        l_in[li].wait_recv()

        def last(r, carry, b=b, ri=ri, li=li):
            here = pl.ds(pl.multiple_of(r * 16, 16), 16)
            there = pl.ds(pl.multiple_of(b * 64 + r * 16, 16), 16)
            out_ref[there, :] = (rr[ri, here, :].astype(F32) + ll[li, here, :].astype(F32)
                                 + part[0, 0, b, here, :].astype(F32)).astype(BF)
            return carry
        lax.fori_loop(0, 4, last, 0)
    for cp in sends:
        cp.wait_send()


def body(queries, keys, values, router_weight, gate_weight, up_weight, down_weight, route_ids):
    tok_dev, width = queries.shape
    block_rows, top_count = route_ids.shape
    dim, hidden = gate_weight.shape[1:]
    anywhere = pl.BlockSpec(memory_space=pl.ANY)
    vmem = pl.BlockSpec(memory_space=pltpu.VMEM)
    V = pltpu.VMEM
    return pl.pallas_call(
        kernel,
        out_shape=jax.ShapeDtypeStruct((block_rows, dim), BF),
        in_specs=[anywhere] * 3 + [vmem] + [anywhere] * 3 + [vmem],
        out_specs=vmem,
        scratch_shapes=[
            V((tok_dev, width), BF), V((tok_dev, width), BF), V((tok_dev, width), BF),
            V((tok_dev, width), F32), V((2, NY * NC, block_rows // 2, width), BF), V((2, NY * NC - 1, block_rows // 2, width), BF),
            V((NZ // 2, 2, 2, block_rows // 2, dim), BF),
            V((NX, 3, UNITS, dim // UNITS, hidden), BF),
            V((2, NX, 4 * CAP, dim), BF), V((NZ // 2, NX * 2 * CAP, dim), BF),
            V((NZ // 2, 2, 2, block_rows // 2, dim), BF),
            V((7, block_rows // 2, dim), BF), V((7, block_rows // 2, dim), BF),
            V((NX, 64, HD), BF), V((NX - 1, 64, HD), BF), V((NX, 64, HD), F32),
            V((64, HD), BF), V((NZ - 1, 64, HD), BF), V((NX - 1, 64, HD), F32), V((NX, 64, HD), F32), V((2, 2 * HD, HD), BF),
            V((NZ, 2 * NX, block_rows), F32), V((NZ, 2 * NX, block_rows), F32),
            pltpu.SemaphoreType.DMA((FLOWS,)), pltpu.SemaphoreType.DMA((FLOWS,)),
            pltpu.SemaphoreType.DMA((8,)),
        ],
        compiler_params=pltpu.CompilerParams(
            collective_id=0, has_side_effects=True, vmem_limit_bytes=62 * 1024 * 1024),
        cost_estimate=pl.CostEstimate(flops=10 ** 10, bytes_accessed=10 ** 7, transcendentals=0),
    )(queries, keys, values, router_weight.T, *(w.reshape(UNITS, dim // UNITS, hidden) for w in (gate_weight, up_weight, down_weight)),
      route_ids.T)


def solution(mesh):
    in_specs = (
        P("seq", "head"),
        P("seq", "head"),
        P("seq", "head"),
        P(),
        P("seq", None, None),
        P("seq", None, None),
        P("seq", None, None),
        P(("seq", "head"), None),
    )
    out_specs = P(("seq", "head"), None)
    return jax.shard_map(body, mesh=mesh, in_specs=in_specs, out_specs=out_specs, check_vma=False)
```

```python
import itertools

import jax
import jax.numpy as jnp
from jax import lax
from jax.experimental import pallas as pl
from jax.experimental.pallas import tpu as pltpu
from jax.sharding import PartitionSpec as P

HD = 128
NX, NZ, NY, NC = 4, 8, 4, 2
CAP = 40
epsilon = 1e-06
BF, F32 = jnp.bfloat16, jnp.float32
MESH = pl.DeviceIdType.MESH
NN, NT, TN = (((1,), (0,)), ((), ())), (((1,), (1,)), ((), ())), (((0,), (0,)), ((), ()))
FLOWS = 192
UNITS, COMMON_U = 32, 2
OWN_U = (UNITS - 2 * COMMON_U) // 4
ORDER = (0, 4, 1, 7, 2, 6, 3, 5)
PIECES = ((0, 0, 3), (0, 3, OWN_U - 3), (1, 0, OWN_U), (2, 0, 4), (2, 4, OWN_U - 4))


def dot(a, b, dims=NN):
    return lax.dot_general(a, b, dims, preferred_element_type=F32)


def kernel(q_hbm, k_hbm, v_hbm, rwt, g_hbm, u_hbm, d_hbm, idst, out_ref,
           qv, kv, vv, att, nrm, landed, tok, wv, xs, ys, part, rr, ll,
           st_out, st_in, tot, zs_out, zs_in, cz_out, cz, car, meta_out, meta_in,
           ssem, rsem, lsem):
    seq, head = lax.axis_index("seq"), lax.axis_index("head")
    z, x = seq // NX, seq % NX
    y, c = head // NC, head % NC
    ids = itertools.count()
    sends = []

    def at_z(k):
        return lax.rem(z + k, NZ) * NX + x

    def at_x(k):
        return z * NX + lax.rem(x + k, NX)

    def at_h(k):
        return lax.rem(head + k, NY * NC)

    def at_y(k):
        return lax.rem(y + k, NY) * NC + c

    other_core = y * NC + (1 - c)

    def push(src, dst, to_seq, to_head):
        i = next(ids)
        cp = pltpu.make_async_remote_copy(
            src_ref=src, dst_ref=dst, send_sem=ssem.at[i], recv_sem=rsem.at[i],
            device_id=(to_seq, to_head), device_id_type=MESH)
        cp.start()
        sends.append(cp)
        return cp

    loads = [pltpu.make_async_copy(src, dst, lsem.at[i])
             for i, (src, dst) in enumerate(((k_hbm, kv), (v_hbm, vv), (q_hbm, qv)))]
    for cp in loads:
        cp.start()
    own = [pltpu.make_async_copy(src, wv.at[0, m], lsem.at[3 + m])
           for m, src in enumerate((g_hbm, u_hbm, d_hbm))]
    for cp in own:
        cp.start()

    barrier = pltpu.get_barrier_semaphore()
    partners = ([(at_x(k), head) for k in range(1, NX)] + [(at_z(k), head) for k in range(1, NZ)]
                + [(seq, at_h(k)) for k in range(1, NY * NC)])
    for to in partners:
        pl.semaphore_signal(barrier, inc=1, device_id=to, device_id_type=MESH)
    pl.semaphore_wait(barrier, len(partners))

    quarter = (2 * lax.rem(y, 2) + c) * OWN_U
    across = (2 * (1 - lax.rem(y, 2)) + c) * OWN_U
    common = 4 * OWN_U + c * COMMON_U
    hbm = (g_hbm, u_hbm, d_hbm)

    def part_of(j, m, start, count):
        return wv.at[j, m, pl.ds(start, count)]

    def same(j, m, start, count, to_seq, to_head):
        piece = part_of(j, m, start, count)
        return push(piece, piece, to_seq, to_head)

    def x_send(m, start, count):
        src = hbm[m].at[pl.ds(start, count)]
        return (push(src, part_of(3, m, start, count), at_x(1), head),
                push(src, part_of(1, m, start, count), at_x(3), head))

    def low(j, i):
        count = PIECES[i][2]
        return count // 2 + (j + i) % 2 * (count % 2)

    def spread(j, i):
        m, first, count = PIECES[i]
        n, start = low(j, i), quarter + first
        return (same(j, m, start, n, seq, at_y(1)), same(j, m, start + n, count - n, seq, at_y(3)),
                same(j, m, start, count, seq, other_core))

    xf, xc, fwd, fwc, spr, cor, com = {}, {}, {}, {}, {}, {}, {}

    def send(i):
        m, first, count = PIECES[i]
        xf[i] = x_send(m, quarter + first, count)

    def do_x(i):
        m, first, count = PIECES[i]
        right, left = xf[i]
        n, start = low(2, i), quarter + first
        right.wait_recv()
        f_right = push(part_of(3, m, start, n), part_of(2, m, start, n), at_x(1), head)
        spr[(3, i)] = spread(3, i)
        left.wait_recv()
        f_left = push(part_of(1, m, start + n, count - n), part_of(2, m, start + n, count - n), at_x(3), head)
        spr[(1, i)] = spread(1, i)
        fwd[i] = (f_right, f_left)

    def do_f(i):
        for cp in fwd[i]:
            cp.wait_recv()
        spr[(2, i)] = spread(2, i)

    def do_y(j, i):
        m, first, count = PIECES[i]
        flows = spr[(j, i)]
        flows[0].wait_recv()
        flows[1].wait_recv()
        cor[(j, i)] = same(j, m, across + first, count, seq, other_core)

    def do_c(m):
        n = COMMON_U // 2
        right, left = xc[m]
        right.wait_recv()
        f_right = push(part_of(3, m, common, n), part_of(2, m, common, n), at_x(1), head)
        left.wait_recv()
        f_left = push(part_of(1, m, common + n, COMMON_U - n), part_of(2, m, common + n, COMMON_U - n), at_x(3), head)
        for j in (3, 1):
            com[(j, m)] = same(j, m, common, COMMON_U, seq, other_core)
        fwc[m] = (f_right, f_left)

    def do_fc(m):
        for cp in fwc[m]:
            cp.wait_recv()
        com[(2, m)] = same(2, m, common, COMMON_U, seq, other_core)

    def ready(j):
        for m in range(3):
            if j == 0:
                own[m].wait()
            else:
                com[(j, m)].wait_recv()
        if j > 0:
            for i in range(len(PIECES)):
                spr[(j, i)][2].wait_recv()
                cor[(j, i)].wait_recv()

    send(0)
    for cp in loads:
        cp.wait()
    for h in range(2):
        cols = slice(h * HD, (h + 1) * HD)
        s = dot(kv[:, cols], vv[:, cols], TN)
        for i in range(2):
            tot[2 * h + i] = s[i * 64:(i + 1) * 64, :]
            st_out[2 * h + i] = s[i * 64:(i + 1) * 64, :].astype(BF)
    st = [push(st_out.at[lax.rem(x + k, NX)], st_in.at[k - 1], at_x(k), head) for k in range(1, NX)]

    def intra(h, tiles):
        cols = slice(h * HD, (h + 1) * HD)
        for i in tiles:
            qi = qv[i * 256:(i + 1) * 256, cols]
            acc = jnp.zeros((256, HD), F32)
            for j in range(i + 1):
                s = dot(qi, kv[j * 256:(j + 1) * 256, cols], NT)
                if i == j:
                    keep = (lax.broadcasted_iota(jnp.int32, (256, 256), 0)
                            >= lax.broadcasted_iota(jnp.int32, (256, 256), 1))
                    s = jnp.where(keep, s, 0.0)
                acc = acc + dot(s.astype(BF), vv[j * 256:(j + 1) * 256, cols])
            att[i * 256:(i + 1) * 256, cols] = acc

    intra(0, (0, 1, 2))
    total = tot[x]
    for k in range(1, NX):
        st[k - 1].wait_recv()
        total = total + st_in[k - 1].astype(F32)
    zs_out[...] = total.astype(BF)
    zs = [push(zs_out, zs_in.at[k - 1], at_z(k), head) for k in range(1, NZ)]
    send(1)
    intra(0, (3,))
    intra(1, (0, 1, 2, 3))
    do_x(0)
    zq = jnp.zeros((64, HD), F32)
    for k in range(1, NZ):
        zs[k - 1].wait_recv()
        zq = zq + zs_in[k - 1].astype(F32) * (z >= k).astype(F32)
    own_state = tot[x]
    for k in range(NX):
        to = lax.rem(x + k, NX)
        entering = zq + own_state * (to > x).astype(F32)
        for i in range(1, NX):
            came_from = lax.rem(x + NX - i, NX)
            entering = entering + st_in[i - 1].astype(F32) * (to > came_from).astype(F32)
        if k == 0:
            cz[x] = entering
        else:
            cz_out[k - 1] = entering
    cs = [push(cz_out.at[k - 1], cz.at[x], at_x(k), head) for k in range(1, NX)]
    do_x(1)
    for cp in cs:
        cp.wait_recv()
    send(2)
    send(3)
    send(4)
    carried = cz[...].reshape(2 * HD, HD)
    high = carried.astype(BF)
    car[0] = high
    car[1] = (carried - high.astype(F32)).astype(BF)

    a2a = {}
    for b in range(2):
        for k in range(NY * NC):
            owned = pl.ds(pl.multiple_of(at_h(k) * 128 + b * 64, 64), 64)
            for h in range(2):
                cols = slice(h * HD, (h + 1) * HD)
                qi = qv[owned, cols]
                a = att[owned, cols] + dot(qi, car[0, cols, :]) + dot(qi, car[1, cols, :])
                scale = lax.rsqrt(jnp.mean(a * a, axis=1, keepdims=True) + epsilon)
                nrm[b, k, :, cols] = (a * scale).astype(BF)
            if k > 0:
                a2a[(b, k)] = push(nrm.at[b, k], landed.at[b, k - 1], seq, at_h(k))

    def assemble(b):
        for k in range(NY * NC):
            if k > 0:
                a2a[(b, k)].wait_recv()
            hcols = pl.ds(pl.multiple_of(lax.rem(head + NY * NC - k, NY * NC) * 2 * HD, 2 * HD), 2 * HD)
            tok[0, 0, b, :, hcols] = nrm[b, 0] if k == 0 else landed[b, k - 1]

    def half(ref, o, b):
        at = ORDER.index(o)
        return ref.at[at // 2, at % 2, b]

    def ag(src, b, right):
        dst = (src + 7) % 8 if right else (src + 1) % 8
        return push(half(tok, src, b), half(tok, dst, b), at_z(1 if right else 7), head)

    ag_r, ag_l = {}, {}
    for b in range(2):
        assemble(b)
        ag_r[(7, b)] = ag(0, b, True)
        ag_l[(1, b)] = ag(0, b, False)

    do_f(0), do_f(1)
    lt = dot(rwt[...], tok[0, 0].reshape(128, rwt.shape[1]), NT)
    experts = lt.shape[0]
    number = lax.broadcasted_iota(jnp.int32, (experts, 128), 0)
    chosen = jnp.zeros((experts, 128), F32)
    for k in range(idst.shape[0]):
        chosen = chosen + jnp.where(number == idst[k:k + 1, :], 1.0, 0.0)
    score = jnp.where(chosen > 0.5, 1.0 / (1.0 + jnp.exp(-lt)), 0.0)
    weight = score / jnp.sum(score, axis=0, keepdims=True)
    earlier = (lax.broadcasted_iota(jnp.int32, (128, 128), 0)
               < lax.broadcasted_iota(jnp.int32, (128, 128), 1))
    rank = dot(chosen.astype(BF), jnp.where(earlier, 1.0, 0.0).astype(BF))
    rank = jnp.where(chosen > 0.5, rank, -1000.0)
    for p in range(NZ):
        meta_out[p, 0:NX, :] = rank[p * NX:(p + 1) * NX, :]
        meta_out[p, NX:2 * NX, :] = weight[p * NX:(p + 1) * NX, :]
    mt = [push(meta_out.at[lax.rem(z + k, NZ)], meta_in.at[8 - k], at_z(k), head) for k in range(1, NZ)]
    meta_in[0] = meta_out[z]

    def forward(o_r, o_l, b):
        ag_r[(o_r, b)].wait_recv()
        if not (o_r == 5 and b == 1):
            ag_r[(o_r - 1, b)] = ag(o_r, b, True)
        ag_l[(o_l, b)].wait_recv()
        if not (o_l == 3 and b == 0):
            ag_l[(o_l + 1, b)] = ag(o_l, b, False)

    slots = 2 * CAP

    def picks(pair, j):
        xj = lax.rem(x + j, NX)
        r0 = meta_in[ORDER[2 * pair], pl.ds(xj, 1), :]
        r1 = meta_in[ORDER[2 * pair + 1], pl.ds(xj, 1), :] + float(CAP)
        r = jnp.concatenate([r0, r1], axis=1)
        return lax.broadcasted_iota(jnp.int32, (slots, 256), 0).astype(F32) == r

    def picked_weight(pair, j):
        xj = lax.rem(x + j, NX)
        w = jnp.concatenate([meta_in[ORDER[2 * pair], pl.ds(NX + xj, 1), :],
                             meta_in[ORDER[2 * pair + 1], pl.ds(NX + xj, 1), :]], axis=1)
        return jnp.sum(jnp.where(picks(pair, j), w, 0.0), axis=1, keepdims=True)

    def all_picks(pair):
        return jnp.concatenate([jnp.where(picks(pair, j), 1.0, 0.0) for j in range(NX)], axis=0).astype(BF)

    def gather(batch, lp, pair):
        p = all_picks(pair)
        for n in range(4):
            cols = slice(n * 512, (n + 1) * 512)
            got = dot(p, tok[pair, :, :, :, cols].reshape(256, 512)).astype(BF)
            for j in range(NX):
                xs[batch, j, lp * slots:(lp + 1) * slots, cols] = got[j * slots:(j + 1) * slots, :]

    def whole(j, m):
        return wv[j, m].reshape(2048, 512)

    def expert(j, batch, first, pairs):
        w = jnp.concatenate([picked_weight(pair, j) for pair in pairs], axis=0)
        rows_in = xs[batch, j, first * slots:(first + len(pairs)) * slots, :]
        gate = dot(rows_in, whole(j, 0))
        up = dot(rows_in, whole(j, 1))
        hidden = (gate / (1.0 + jnp.exp(-gate)) * up * w).astype(BF)
        for n in range(4):
            cols = slice(n * 512, (n + 1) * 512)
            made = dot(hidden, wv[j, 2, n * 8:(n + 1) * 8].reshape(512, 512), NT).astype(BF)
            for lp, pair in enumerate(pairs):
                ys[pair, j * slots:(j + 1) * slots, cols] = made[lp * slots:(lp + 1) * slots, :]

    def combine(pair):
        p = all_picks(pair)
        for n in range(4):
            cols = slice(n * 512, (n + 1) * 512)
            part[pair, :, :, :, cols] = dot(p, ys[pair, :, cols], TN).astype(BF).reshape(2, 2, 64, 512)

    near, middle, last = (1, 2), (3,), (0,)
    do_x(2)
    forward(7, 1, 0)
    for cp in mt:
        cp.wait_recv()
    do_x(3)
    forward(7, 1, 1)
    do_x(4)
    for m in range(3):
        xc[m] = x_send(m, common, COMMON_U)
    gather(0, 0, 1)
    forward(6, 2, 0)
    for i in (0, 1):
        do_y(3, i), do_y(1, i), do_y(2, i)
    do_f(2)
    forward(6, 2, 1)
    gather(0, 1, 2)
    ready(0)
    do_f(3)
    do_f(4)
    expert(0, 0, 0, near)
    forward(5, 3, 0)
    do_y(3, 2), do_y(1, 2)
    do_c(0), do_c(1)
    forward(5, 3, 1)
    do_c(2)
    gather(1, 0, 3)
    for i in (3, 4):
        do_y(3, i), do_y(1, i)
    expert(0, 1, 0, middle)
    ready(3)
    expert(3, 1, 0, middle)
    do_y(2, 2)
    do_fc(0), do_fc(1)
    expert(3, 0, 0, near)
    ready(1)
    expert(1, 1, 0, middle)
    do_fc(2)
    do_y(2, 3), do_y(2, 4)
    expert(1, 0, 0, near)
    ready(2)
    expert(2, 1, 0, middle)
    combine(3)

    def fold(buf, i, o, b):
        def step(r, carry):
            here = pl.ds(pl.multiple_of(r * 16, 16), 16)
            buf[i, here, :] = (buf[i, here, :].astype(F32) + part[ORDER.index(o) // 2, ORDER.index(o) % 2, b, here, :].astype(F32)).astype(BF)
            return carry
        lax.fori_loop(0, 4, step, 0)

    order = ((3, 1), (4, 0), (2, 1), (3, 0), (1, 1), (2, 0), (1, 0))
    r_in, l_in = {}, {}

    def begin(i):
        o, b = order[i]
        r_in[i] = push(half(part, o, b), rr.at[i], at_z(1), head)
        l_in[i] = push(half(part, 8 - o, 1 - b), ll.at[i], at_z(7), head)

    def onward(i):
        o, b = order[i]
        came = order.index((o + 1, b))
        r_in[came].wait_recv()
        fold(rr, came, o, b)
        r_in[i] = push(rr.at[came], rr.at[i], at_z(1), head)
        l_in[came].wait_recv()
        fold(ll, came, 8 - o, 1 - b)
        l_in[i] = push(ll.at[came], ll.at[i], at_z(7), head)

    begin(0)
    ag_r[(4, 0)].wait_recv()
    ag_l[(4, 1)].wait_recv()
    gather(1, 1, 0)
    for j in range(NX):
        expert(j, 1, 1, last)
    combine(0)
    begin(1)
    expert(2, 0, 0, near)
    combine(2)
    onward(2)
    combine(1)
    for i in range(3, 7):
        onward(i)
    for b, (ri, li) in enumerate(((6, 4), (4, 6))):
        r_in[ri].wait_recv()
        l_in[li].wait_recv()

        def last(r, carry, b=b, ri=ri, li=li):
            here = pl.ds(pl.multiple_of(r * 16, 16), 16)
            there = pl.ds(pl.multiple_of(b * 64 + r * 16, 16), 16)
            out_ref[there, :] = (rr[ri, here, :].astype(F32) + ll[li, here, :].astype(F32)
                                 + part[0, 0, b, here, :].astype(F32)).astype(BF)
            return carry
        lax.fori_loop(0, 4, last, 0)
    for cp in sends:
        cp.wait_send()


def body(queries, keys, values, router_weight, gate_weight, up_weight, down_weight, route_ids):
    tok_dev, width = queries.shape
    block_rows, top_count = route_ids.shape
    dim, hidden = gate_weight.shape[1:]
    anywhere = pl.BlockSpec(memory_space=pl.ANY)
    vmem = pl.BlockSpec(memory_space=pltpu.VMEM)
    V = pltpu.VMEM
    return pl.pallas_call(
        kernel,
        out_shape=jax.ShapeDtypeStruct((block_rows, dim), BF),
        in_specs=[anywhere] * 3 + [vmem] + [anywhere] * 3 + [vmem],
        out_specs=vmem,
        scratch_shapes=[
            V((tok_dev, width), BF), V((tok_dev, width), BF), V((tok_dev, width), BF),
            V((tok_dev, width), F32), V((2, NY * NC, block_rows // 2, width), BF), V((2, NY * NC - 1, block_rows // 2, width), BF),
            V((NZ // 2, 2, 2, block_rows // 2, dim), BF),
            V((NX, 3, UNITS, dim // UNITS, hidden), BF),
            V((2, NX, 4 * CAP, dim), BF), V((NZ // 2, NX * 2 * CAP, dim), BF),
            V((NZ // 2, 2, 2, block_rows // 2, dim), BF),
            V((7, block_rows // 2, dim), BF), V((7, block_rows // 2, dim), BF),
            V((NX, 64, HD), BF), V((NX - 1, 64, HD), BF), V((NX, 64, HD), F32),
            V((64, HD), BF), V((NZ - 1, 64, HD), BF), V((NX - 1, 64, HD), F32), V((NX, 64, HD), F32), V((2, 2 * HD, HD), BF),
            V((NZ, 2 * NX, block_rows), F32), V((NZ, 2 * NX, block_rows), F32),
            pltpu.SemaphoreType.DMA((FLOWS,)), pltpu.SemaphoreType.DMA((FLOWS,)),
            pltpu.SemaphoreType.DMA((8,)),
        ],
        compiler_params=pltpu.CompilerParams(
            collective_id=0, has_side_effects=True, vmem_limit_bytes=62 * 1024 * 1024),
        cost_estimate=pl.CostEstimate(flops=10 ** 10, bytes_accessed=10 ** 7, transcendentals=0),
    )(queries, keys, values, router_weight.T, *(w.reshape(UNITS, dim // UNITS, hidden) for w in (gate_weight, up_weight, down_weight)),
      route_ids.T)


def solution(mesh):
    in_specs = (
        P("seq", "head"),
        P("seq", "head"),
        P("seq", "head"),
        P(),
        P("seq", None, None),
        P("seq", None, None),
        P("seq", None, None),
        P(("seq", "head"), None),
    )
    out_specs = P(("seq", "head"), None)
    return jax.shard_map(body, mesh=mesh, in_specs=in_specs, out_specs=out_specs, check_vma=False)
```
